256 devices in a mesh: outer: 32 (over z, y_hi, core), inner: 8 (over x, y_lo).
Axes of the slice: x: 4, y: 4 (y_hi: 2, y_lo: 2; y = y_hi * 2 + y_lo), z: 8, core: 2. Of those that a mesh axis runs over, the one named last changes fastest.
Arguments:
- image_emb: bfloat16 [131072, 1152], P(('outer', 'inner'))
- text_emb: bfloat16 [131072, 1152], P(('outer', 'inner'))
- positive: int32 [131072], P(('outer', 'inner')), may hold values from 0 to 131071, as said below
- log_temp: float32 [1], replicated, may hold values from 1 to 2
- bias: float32 [1], replicated, may hold values from -3 to -1
Outputs:
- loss: float32 [1], replicated
- grad_image: float32 [131072, 1152], P(('outer', 'inner'))
- grad_text: float32 [131072, 1152], P(('outer', 'inner'))
The draws below stay inside these ranges and needn't reach their ends.
Inputs may be any that keep to these rules, and one draw needn't show every extreme that they name: positive maps each aligned block of 512 rows one to one onto the text indices of the same block.
All inputs are finite; a program needn't handle non-finite values.
Results may differ from the reference program's by a relative error of at most 0.00033.
Values may be sent and summed in bfloat16 or wider, within the bound.
A program may use at most 64 MiB of HBM per device.

```python
import jax
import jax.numpy as jnp
from jax import lax

D = 1152
TOK_DEV = 512
TOKENS = 131072
N_OUTER = 32
N_INNER = 8


def common_direction(key):
    return jax.random.normal(key, (D,), jnp.float32)


def embedding_rows(key, top):
    groups = TOKENS // TOK_DEV
    noise = jax.random.normal(key, (TOKENS, D), jnp.float32)
    block = (jnp.arange(TOKENS, dtype=jnp.int32) // TOK_DEV).astype(jnp.float32)
    weight = top * block / max(groups - 1, 1)
    return (noise, weight)


def draw_image_emb(key, part):
    direction = common_direction(key)
    key = jax.random.fold_in(key, 21)
    noise, weight = embedding_rows(key, 1.5)
    return (0.03 * (noise + weight[:, None] * direction[None, :])).astype(jnp.bfloat16)


def draw_text_emb(key, part):
    direction = common_direction(key)
    key = jax.random.fold_in(key, 22)
    noise, weight = embedding_rows(key, 1.5)
    return (0.03 * (noise + weight[:, None] * direction[None, :])).astype(jnp.bfloat16)


def draw_positive(key, part):
    key = jax.random.fold_in(key, 11)
    groups = TOKENS // TOK_DEV
    keys = jax.random.split(key, groups)
    perms = jax.vmap(lambda k: jax.random.permutation(k, TOK_DEV))(keys).astype(jnp.int32)
    offsets = (jnp.arange(groups, dtype=jnp.int32) * TOK_DEV)[:, None]
    return (perms + offsets).reshape(TOKENS)


def setup_inputs(seed: int = 0) -> dict:
    arg_keys = jax.random.split(jax.random.key(seed), 6)
    return {
        "image_emb": draw_image_emb(jax.random.fold_in(arg_keys[5], 71), 0),
        "text_emb": draw_text_emb(jax.random.fold_in(arg_keys[5], 71), 0),
        "positive": draw_positive(jax.random.fold_in(arg_keys[5], 71), 0),
        "log_temp": jnp.clip(jax.random.uniform(arg_keys[3], (1,), jnp.float32, 1.0, 2.0), 1.0, 2.0),
        "bias": jnp.clip(jax.random.uniform(arg_keys[4], (1,), jnp.float32, -3.0, -1.0), -3.0, -1.0),
    }


HOPS = ((0, 0), (0, 1), (0, 2), (0, 3), (1, 3))

def normalize(x):
    xf = x.astype(jnp.float32)
    inv = lax.rsqrt(lax.optimization_barrier(jnp.sum(xf * xf, axis=1, keepdims=True)) + 1e-06)
    return (xf * inv, inv)

def tile_terms(z_img, z_txt, text_block, pos_rows, temp, shift_b):
    rows = z_txt.shape[0]
    scores = jnp.einsum('bd,cd->bc', z_img.astype(jnp.float32), z_txt.astype(jnp.float32))
    logit = temp * scores + shift_b
    columns = text_block * rows + jnp.arange(rows, dtype=jnp.int32)
    label = (pos_rows[:, None] == columns[None, :]).astype(jnp.float32)
    term = jnp.sum(jax.nn.softplus(-(2.0 * label - 1.0) * logit))
    coef = (jax.nn.sigmoid(logit) - label).astype(jnp.bfloat16)
    d_img = jnp.dot(coef, z_txt, preferred_element_type=jnp.float32)
    d_txt = jnp.einsum('bc,bd->cd', coef.astype(jnp.float32), z_img.astype(jnp.float32))
    return (term, d_img, d_txt)

def reference(image_emb, text_emb, positive, log_temp, bias):
    groups = N_OUTER * N_INNER
    temp = jnp.exp(log_temp[0])
    shift_b = bias[0]
    zn_img, inv_img = normalize(image_emb)
    zn_txt, inv_txt = normalize(text_emb)
    zi_blocks = zn_img.astype(jnp.bfloat16).reshape(groups, TOK_DEV, D)
    zt_blocks = zn_txt.astype(jnp.bfloat16).reshape(N_OUTER, N_INNER, TOK_DEV, D)
    pos_blocks = positive.reshape(groups, TOK_DEV)
    block_ids = jnp.arange(groups, dtype=jnp.int32).reshape(N_OUTER, N_INNER)
    d_image = jnp.zeros((groups, TOK_DEV, D), jnp.float32)
    d_text = jnp.zeros((N_OUTER, N_INNER, TOK_DEV, D), jnp.float32)
    total = jnp.zeros((), jnp.float32)

    def one(items):
        return tile_terms(items[0], items[1], items[2], items[3], temp, shift_b)
    for hop in HOPS:
        rolled = jnp.roll(zt_blocks, hop, axis=(0, 1)).reshape(groups, TOK_DEV, D)
        ids = jnp.roll(block_ids, hop, axis=(0, 1)).reshape(groups)
        terms, d_img, d_txt = lax.map(one, (zi_blocks, rolled, ids, pos_blocks))
        total = total + jnp.sum(terms)
        d_image = d_image + d_img
        back = (-hop[0], -hop[1])
        d_text = d_text + jnp.roll(d_txt.reshape(N_OUTER, N_INNER, TOK_DEV, D), back, axis=(0, 1))
    d_image = temp * d_image.reshape(TOKENS, D)
    d_text = temp * d_text.reshape(TOKENS, D)
    grad_image = (d_image - zn_img * lax.optimization_barrier(jnp.sum(zn_img * d_image, axis=1, keepdims=True))) * inv_img
    grad_text = (d_text - zn_txt * lax.optimization_barrier(jnp.sum(zn_txt * d_text, axis=1, keepdims=True))) * inv_txt
    loss = jnp.reshape(total / TOKENS, (1,))
    return (loss, grad_image, grad_text)
```

```python
import functools

import jax
import jax.numpy as jnp
from jax import lax
from jax.experimental import pallas as pl
from jax.experimental.pallas import tpu as pltpu
from jax.sharding import PartitionSpec as P

MESH = pl.DeviceIdType.MESH
CHUNK = 64
STEP = 128
TILE = 256


def kernel(
    image, text, positive_hbm, log_temp, bias, loss, g_image, g_text,
    z, raw, d, inv, acc, terms, positive, load_sem, send_sem, recv_sem, loss_send, loss_recv,
):
    rows, width = image.shape
    chunks = rows // CHUNK
    n_outer, n_inner = lax.axis_size("outer"), lax.axis_size("inner")
    o, i = lax.axis_index("outer"), lax.axis_index("inner")
    p, core = lax.rem(i, 2), lax.rem(o, 2)

    def along(steps):
        return (o, lax.rem(i + steps + n_inner, n_inner))

    partner = (o, i + 1 - 2 * p)

    def across(side):
        return (
            lax.rem(o + 1 - 2 * side + n_outer, n_outer),
            lax.rem(i + core - side + n_inner, n_inner),
        )

    barrier = pltpu.get_barrier_semaphore()
    others = (along(2), along(-2), partner, across(0), across(1))

    group = 2 * n_inner
    pairs = n_outer // 2

    def near(k):
        m = lax.rem(2 * i + core + k, group)
        return (o - core + lax.rem(m, 2), m // 2)

    def far(k):
        return (lax.rem(o + 2 * k, n_outer), i)

    def loop(lower, upper, step):
        lax.fori_loop(lower, upper, lambda k, carry: (step(k), carry)[1], 0)

    def greet(device):
        pl.semaphore_signal(barrier, inc=1, device_id=device, device_id_type=MESH)

    for other in others:
        greet(other)
    loop(1, group, lambda k: greet(near(k)))
    loop(1, pairs, lambda k: greet(far(k)))
    n_greet = len(others) + group - 1 + pairs - 1

    def loading(side, c):
        source = image if side else text
        span = pl.ds(c * CHUNK, CHUNK)
        return pltpu.make_async_copy(source.at[span], raw.at[side, span], load_sem.at[side, c])

    for c in range(chunks):
        for side in (0, 1):
            loading(side, c).start()
    load_positive = pltpu.make_async_copy(positive_hbm, positive, load_sem.at[2, 0])
    load_positive.start()

    def copy(side, source, target, c, kind, device):
        span = pl.ds(c * CHUNK, CHUNK)
        return pltpu.make_async_remote_copy(
            src_ref=z.at[side, source, span],
            dst_ref=z.at[side, target, span],
            send_sem=send_sem.at[side, kind],
            recv_sem=recv_sem.at[side, target, c],
            device_id=device,
            device_id_type=MESH,
        )

    def send_ring(side, c):
        copy(side, 0, 2, c, 0, along(2 - 4 * side)).start()

    def send_partner(side, source, c):
        copy(side, source, 1, c, 1, partner).start()

    def send_on(side, c):
        copy(side, 1, 3, c, 2, along(2 - 4 * side)).start()

    def send_cross(side, source, c):
        copy(side, source, 4, c, 3, across(side)).start()

    def arrived(side, slot, c):
        copy(side, slot, slot, c, 0, partner).wait_recv()

    def normalize(side, c):
        span = pl.ds(c * CHUNK, CHUNK)
        x = raw[side, span].astype(jnp.float32)
        scale = lax.rsqrt(jnp.sum(x * x, axis=1, keepdims=True) + 1e-06)
        inv[side, span] = jnp.broadcast_to(scale, (CHUNK, 128))
        z[side, 0, span] = (x * scale).astype(jnp.bfloat16)

    for c in range(chunks):
        for side in (0, 1):
            loading(side, c).wait()
            normalize(side, c)
            if c == 0 and side == 0:
                pl.semaphore_wait(barrier, n_greet)
            send_ring(side, c)

            @pl.when(p == side)
            def _():
                send_partner(side, 0, c)

    temp = jnp.exp(jnp.full((1, 128), log_temp[0], jnp.float32))[:, :1]
    shift = bias[0]

    def sigmoid_parts(logit):
        e = jnp.exp(-jnp.abs(logit))
        r = 1.0 / (1.0 + e)
        return e, jnp.where(logit >= 0.0, r, e * r)

    def fold(term):
        return jnp.sum(term.reshape(-1, 8, term.shape[1]), axis=0)

    def term_copy(stage, k, device):
        return pltpu.make_async_remote_copy(
            src_ref=terms.at[stage, 0], dst_ref=terms.at[stage, k],
            send_sem=loss_send.at[stage], recv_sem=loss_recv.at[stage],
            device_id=device, device_id_type=MESH,
        )

    def spread(stage, value, count, where):
        terms[stage, 0] = value
        loop(1, count, lambda k: term_copy(stage, k, where(k)).start())

    def gathered(stage, count):
        block = terms.at[stage, pl.ds(1, count - 1)]
        both = pltpu.make_async_remote_copy(
            src_ref=block, dst_ref=block, send_sem=loss_send.at[stage], recv_sem=loss_recv.at[stage],
            device_id=partner, device_id_type=MESH,
        )
        both.wait_recv()
        both.wait_send()
        return jnp.sum(terms[stage, :count], axis=0)

    base = (o * n_inner + i) * rows
    acc[...] = jnp.zeros_like(acc)
    load_positive.wait()

    def own_tile(n, carry):
        span = pl.ds(pl.multiple_of(n * STEP, STEP), STEP)
        scores = lax.dot_general(
            z[0, 0, span], z[1, 0], (((1,), (1,)), ((), ())), preferred_element_type=jnp.float32
        )
        logit = temp * scores + shift
        label = positive[...] - (base + n * STEP) == lax.broadcasted_iota(jnp.int32, scores.shape, 0)
        e, sig = sigmoid_parts(logit)
        term = jnp.maximum(logit, 0.0) + jnp.log1p(e) - jnp.where(label, logit, 0.0)
        folded = fold(term)
        acc[...] += sum(folded[:, k * STEP:(k + 1) * STEP] for k in range(rows // STEP))
        coef = (sig - label.astype(jnp.float32)).astype(jnp.bfloat16)
        d[0, span] = jnp.dot(coef, z[1, 0], preferred_element_type=jnp.float32)
        add = lax.dot_general(
            coef, z[0, 0, span], (((0,), (0,)), ((), ())), preferred_element_type=jnp.float32
        )

        @pl.when(n == 0)
        def _():
            d[1] = add

        @pl.when(n > 0)
        def _():
            d[1] += add

        return carry

    lax.fori_loop(0, rows // STEP, own_tile, 0)

    def tile(side, slot, n):
        span = pl.ds(pl.multiple_of(n * STEP, STEP), STEP)
        weight = jnp.where(side == 0, 1.0, 0.0)

        def part(k, carry):
            own = pl.ds(pl.multiple_of(k * TILE, TILE), TILE)
            scores = lax.dot_general(
                z[1 - side, 0, own], z[side, slot, span], (((1,), (1,)), ((), ())),
                preferred_element_type=jnp.float32,
            )
            logit = temp * scores + shift
            e, sig = sigmoid_parts(logit)
            acc[...] += weight * fold(jnp.maximum(logit, 0.0) + jnp.log1p(e))
            d[1 - side, own] += jnp.dot(
                sig.astype(jnp.bfloat16), z[side, slot, span], preferred_element_type=jnp.float32
            )
            return carry

        lax.fori_loop(0, rows // TILE, part, 0)

    per = STEP // CHUNK

    def take_ring(side, c):
        arrived(side, 2, c)

        @pl.when(p != side)
        def _():
            send_partner(side, 2, c)

        @pl.when(core != side)
        def _():
            send_cross(side, 2, c)

    def take_last(side, c):
        arrived(side, 3, c)

        @pl.when(core == side)
        def _():
            send_cross(side, 3, c)

    def take_partner(side, c):
        arrived(side, 1, c)
        send_on(side, c)

    early, late = 1 - p, p

    def first(n, carry):
        for k in range(per):
            c = n * per + k
            take_ring(0, c)
            take_ring(1, c)
            take_partner(early, c)
        tile(0, 2, n)
        tile(1, 2, n)
        tile(early, 1, n)
        return carry

    lax.fori_loop(0, rows // STEP, first, 0)

    def second(n, carry):
        for k in range(per):
            c = n * per + k
            take_partner(late, c)
            take_last(early, c)
        tile(late, 1, n)
        tile(early, 3, n)
        for k in range(per):
            c = n * per + k
            take_last(late, c)
        tile(late, 3, n)
        for side in (0, 1):
            for k in range(per):
                arrived(side, 4, n * per + k)
            tile(side, 4, n)
            if side == 0:

                @pl.when(n == rows // STEP - 1)
                def _():
                    spread(0, acc[...], group, near)

        return carry

    lax.fori_loop(0, rows // STEP, second, 0)

    spread(1, gathered(0, group), pairs, far)

    def finish(c, carry):
        span = pl.ds(pl.multiple_of(c * CHUNK, CHUNK), CHUNK)
        for side, out in ((0, g_text), (1, g_image)):
            scale = inv[side, span][:, :1]
            zn = raw[side, span].astype(jnp.float32) * scale
            grad = temp * d[side, span]
            out[span] = (grad - zn * jnp.sum(zn * grad, axis=1, keepdims=True)) * scale
        return carry

    lax.fori_loop(0, chunks, finish, 0)

    for side in (0, 1):
        for kind in range(4):
            pltpu.make_async_remote_copy(
                src_ref=z.at[side, 0], dst_ref=z.at[side, 0],
                send_sem=send_sem.at[side, kind], recv_sem=recv_sem.at[side, 0, 0],
                device_id=partner, device_id_type=MESH,
            ).wait_send()

    loss[0] = jnp.sum(gathered(1, pairs)) / (rows * n_outer * n_inner)


def body(image_emb, text_emb, positive, log_temp, bias):
    rows, width = image_emb.shape
    chunks = rows // CHUNK
    vmem, smem, anywhere = (pl.BlockSpec(memory_space=m) for m in (pltpu.VMEM, pltpu.SMEM, pl.ANY))
    flops = 2 * 19 * rows * rows * width
    return pl.pallas_call(
        kernel,
        out_shape=(
            jax.ShapeDtypeStruct((1,), jnp.float32),
            jax.ShapeDtypeStruct((rows, width), jnp.float32),
            jax.ShapeDtypeStruct((rows, width), jnp.float32),
        ),
        in_specs=[anywhere, anywhere, anywhere, smem, smem],
        out_specs=(smem, vmem, vmem),
        scratch_shapes=[
            pltpu.VMEM((2, 5, rows, width), jnp.bfloat16),
            pltpu.VMEM((2, rows, width), jnp.bfloat16),
            pltpu.VMEM((2, rows, width), jnp.float32),
            pltpu.VMEM((2, rows, 128), jnp.float32),
            pltpu.VMEM((8, STEP), jnp.float32),
            pltpu.VMEM((2, 16, 8, STEP), jnp.float32),
            pltpu.VMEM((1, rows), jnp.int32),
            pltpu.SemaphoreType.DMA((3, chunks)),
            pltpu.SemaphoreType.DMA((2, 4)),
            pltpu.SemaphoreType.DMA((2, 5, chunks)),
            pltpu.SemaphoreType.DMA((2,)),
            pltpu.SemaphoreType.DMA((2,)),
        ],
        compiler_params=pltpu.CompilerParams(
            collective_id=0, has_side_effects=True, vmem_limit_bytes=60 * 2**20
        ),
        cost_estimate=pl.CostEstimate(
            flops=flops, bytes_accessed=12 * rows * width, transcendentals=27 * rows * rows
        ),
        name="exchange",
    )(image_emb, text_emb, positive.reshape(1, rows), log_temp, bias)


def solution(mesh):
    placed = (
        P(("outer", "inner"), None),
        P(("outer", "inner"), None),
        P(("outer", "inner")),
        P(),
        P(),
    )
    return jax.shard_map(
        body,
        mesh=mesh,
        in_specs=placed,
        out_specs=(P(), P(("outer", "inner"), None), P(("outer", "inner"), None)),
        check_vma=False,
    )
```

```python
import functools

import jax
import jax.numpy as jnp
from jax import lax
from jax.experimental import pallas as pl
from jax.experimental.pallas import tpu as pltpu
from jax.sharding import PartitionSpec as P

MESH = pl.DeviceIdType.MESH
CHUNK = 64
WIDE, NARROW = 256, 128
HELD = 2
SPLIT = 4


def kernel(
    image, text, positive_hbm, log_temp, bias, loss, g_image, g_text,
    z, raw, d, inv, acc, terms, positive, load_sem, send_sem, recv_sem, loss_send, loss_recv,
):
    rows, width = image.shape
    chunks = rows // CHUNK
    n_outer, n_inner = lax.axis_size("outer"), lax.axis_size("inner")
    o, i = lax.axis_index("outer"), lax.axis_index("inner")
    p, core = lax.rem(i, 2), lax.rem(o, 2)

    def along(steps):
        return (o, lax.rem(i + steps + n_inner, n_inner))

    partner = (o, i + 1 - 2 * p)

    def across(side):
        return (
            lax.rem(o + 1 - 2 * side + n_outer, n_outer),
            lax.rem(i + core - side + n_inner, n_inner),
        )

    barrier = pltpu.get_barrier_semaphore()
    sibling = (o + 1 - 2 * core, i)
    beside = (lax.rem(o + 2 * core - 1 + n_outer, n_outer), i)
    others = (along(2), along(-2), partner, across(0), across(1), beside, sibling)

    group = 2 * n_inner
    pairs = n_outer // 2

    def near(k):
        m = lax.rem(2 * i + core + k, group)
        return (o - core + lax.rem(m, 2), m // 2)

    def far(k):
        return (lax.rem(o + 2 * k, n_outer), i)

    def loop(lower, upper, step):
        lax.fori_loop(lower, upper, lambda k, carry: (step(k), carry)[1], 0)

    def greet(device):
        pl.semaphore_signal(barrier, inc=1, device_id=device, device_id_type=MESH)

    for other in others:
        greet(other)
    loop(1, group, lambda k: greet(near(k)))
    loop(1, pairs, lambda k: greet(far(k)))
    n_greet = len(others) + group - 1 + pairs - 1

    def loading(side, c):
        source = image if side else text
        span = pl.ds(c * CHUNK, CHUNK)
        return pltpu.make_async_copy(source.at[span], raw.at[side, span], load_sem.at[side, c])

    for c in range(chunks):
        for side in (0, 1):
            loading(side, c).start()
    load_positive = pltpu.make_async_copy(positive_hbm, positive, load_sem.at[2, 0])
    load_positive.start()

    def copy(side, source, target, c, kind, device):
        span = pl.ds(c * CHUNK, CHUNK)
        return pltpu.make_async_remote_copy(
            src_ref=z.at[side, source, span],
            dst_ref=z.at[side, target, span],
            send_sem=send_sem.at[side, kind],
            recv_sem=recv_sem.at[side, target, c],
            device_id=device,
            device_id_type=MESH,
        )

    def send_ring(side, c):
        copy(side, 0, 2, c, 0, along(2 - 4 * side)).start()

    def send_partner(side, source, c):
        copy(side, source, 1, c, 1, partner).start()

    def send_on(side, c):
        copy(side, 1, 3, c, 2, along(2 - 4 * side)).start()

    def send_cross(side, source, c):
        copy(side, source, 4, c, 3, across(side)).start()

    def send_beside(side, c):
        copy(side, 3, 4, c, 4, beside).start()

    def send_sibling(c):
        copy(0, 1, 5, c, 5, sibling).start()

    def arrived(side, slot, c):
        copy(side, slot, slot, c, 0, partner).wait_recv()

    def normalize(side, c):
        span = pl.ds(c * CHUNK, CHUNK)
        x = raw[side, span].astype(jnp.float32)
        scale = lax.rsqrt(jnp.sum(x * x, axis=1, keepdims=True) + 1e-06)
        inv[side, span] = jnp.broadcast_to(scale, (CHUNK, 128))
        z[side, 0, span] = (x * scale).astype(jnp.bfloat16)

    for c in range(chunks):
        for side in (0, 1):
            loading(side, c).wait()
            normalize(side, c)
            if c == 0 and side == 0:
                pl.semaphore_wait(barrier, n_greet)
            send_ring(side, c)
            if side == 0 or c < HELD:

                @pl.when(p == side)
                def _():
                    send_partner(side, 0, c)

    load_positive.wait()
    temp = jnp.exp(jnp.full((1, 128), log_temp[0], jnp.float32))[:, :1]
    shift = bias[0]

    def sigmoid_parts(logit):
        e = jnp.exp(-jnp.abs(logit))
        r = 1.0 / (1.0 + e)
        return e, jnp.where(logit >= 0.0, r, e * r)

    def fold(term):
        rest = jnp.sum(term.reshape(-1, 8, term.shape[1]), axis=0)
        return sum(rest[:, k:k + 128] for k in range(0, term.shape[1], 128))

    def term_copy(stage, k, device):
        return pltpu.make_async_remote_copy(
            src_ref=terms.at[stage, 0], dst_ref=terms.at[stage, k],
            send_sem=loss_send.at[stage], recv_sem=loss_recv.at[stage],
            device_id=device, device_id_type=MESH,
        )

    def spread(stage, value, count, where):
        terms[stage, 0] = value
        loop(1, count, lambda k: term_copy(stage, k, where(k)).start())

    def gathered(stage, count):
        block = terms.at[stage, pl.ds(1, count - 1)]
        both = pltpu.make_async_remote_copy(
            src_ref=block, dst_ref=block, send_sem=loss_send.at[stage], recv_sem=loss_recv.at[stage],
            device_id=partner, device_id_type=MESH,
        )
        both.wait_recv()
        both.wait_send()
        return jnp.sum(terms[stage, :count], axis=0)

    base = (o * n_inner + i) * rows
    acc[...] = jnp.zeros_like(acc)

    def own_tile(n, carry):
        span = pl.ds(pl.multiple_of(n * WIDE, WIDE), WIDE)
        scores = lax.dot_general(
            z[0, 0, span], z[1, 0], (((1,), (1,)), ((), ())), preferred_element_type=jnp.float32
        )
        logit = temp * scores + shift
        label = positive[...] - (base + n * WIDE) == lax.broadcasted_iota(jnp.int32, scores.shape, 0)
        e, sig = sigmoid_parts(logit)
        term = jnp.maximum(logit, 0.0) + jnp.log1p(e) - jnp.where(label, logit, 0.0)
        acc[...] += fold(term)
        coef = (sig - label.astype(jnp.float32)).astype(jnp.bfloat16)
        d[0, span] = jnp.dot(coef, z[1, 0], preferred_element_type=jnp.float32)
        add = lax.dot_general(
            coef, z[0, 0, span], (((0,), (0,)), ((), ())), preferred_element_type=jnp.float32
        )

        @pl.when(n == 0)
        def _():
            d[1] = add

        @pl.when(n > 0)
        def _():
            d[1] += add

        return carry

    lax.fori_loop(0, rows // WIDE, own_tile, 0)

    def softplus(logit, e):
        return fold(jnp.maximum(logit, 0.0) + jnp.log1p(e))

    def tile(side, slot, n, size, weight=None):
        span = pl.ds(pl.multiple_of(n * size, size), size)
        scores = lax.dot_general(
            z[1 - side, 0], z[side, slot, span], (((1,), (1,)), ((), ())),
            preferred_element_type=jnp.float32,
        )
        logit = temp * scores + shift
        e, sig = sigmoid_parts(logit)
        if weight is not None:
            acc[...] += weight * softplus(logit, e)
        d[1 - side] += jnp.dot(
            sig.astype(jnp.bfloat16), z[side, slot, span], preferred_element_type=jnp.float32
        )

    def loss_tile(slot, n):
        span = pl.ds(pl.multiple_of(n * WIDE, WIDE), WIDE)
        scores = lax.dot_general(
            z[1, 2], z[0, slot, span], (((1,), (1,)), ((), ())), preferred_element_type=jnp.float32
        )
        logit = temp * scores + shift
        acc[...] += softplus(logit, jnp.exp(-jnp.abs(logit)))

    def take_ring(side, c):
        arrived(side, 2, c)

        @pl.when(p != side)
        def _():
            send_partner(side, 2, c)

        @pl.when((core != side) & ((p == side) | (c >= SPLIT)))
        def _():
            send_cross(side, 2, c)

    def take_last(side, c):
        arrived(side, 3, c)

        @pl.when(core == side)
        def _():
            send_cross(side, 3, c)

        @pl.when((core != side) & (p == side) & (c < SPLIT))
        def _():
            send_beside(side, c)

    def take_partner(side, c):
        arrived(side, 1, c)
        send_on(side, c)

    per = NARROW // CHUNK
    steps = rows // NARROW
    wide = rows // WIDE

    def take_text(c):
        take_partner(0, c)

        @pl.when(core == 0)
        def _():
            send_sibling(c)

    @functools.partial(loop, 0, steps)
    def _(n):
        for k in range(per):
            c = n * per + k
            take_ring(0, c)
            take_ring(1, c)

            @pl.when(c > 0)
            def _():
                take_text(c - 1)

        @pl.when(n == steps - 1)
        def _():
            @pl.when(p == 1)
            def _():
                loop(HELD, chunks, lambda c: send_partner(1, 0, c))

        @pl.when(lax.rem(n, steps // wide) == steps // wide - 1)
        def _():
            tile(0, 2, n // (steps // wide), WIDE, 1.0)
            tile(1, 2, n // (steps // wide), WIDE)

        @pl.when(n == steps // wide)
        def _():
            tile(0, 1, 0, WIDE, 1.0)

    take_text(chunks - 1)

    def plain(n, j):
        side, slot = jnp.where(j == 1, 0, 1), jnp.where(j == 0, 1, 3)

        @pl.when(((j == 2) & (n > 0)) | ((j < 2) & (n < steps)))
        def _():
            tile(side, slot, n - j // 2, NARROW)

    def crossing(side, n, weight=None):
        n = jnp.where(core == side, lax.rem(n + SPLIT // per, steps), n)
        for k in range(per):
            arrived(side, 4, n * per + k)
        tile(side, 4, n, NARROW, weight)

    @functools.partial(loop, 0, steps + 1)
    def _(n):
        @pl.when(n == steps)
        def _():
            spread(1, gathered(0, group), pairs, far)

        for k in range(per):
            c = n * per + k

            @pl.when(n < steps)
            def _():
                take_partner(1, c)
                take_last(0, c)

            @pl.when(n > 0)
            def _():
                take_last(1, c - per)

            if k == 0:

                @pl.when((n >= core) & (n < steps + core))
                def _():
                    crossing(0, n - core, 1.0 - core.astype(jnp.float32))

                @pl.when(n == steps - 1)
                def _():
                    spread(0, acc[...], group, near)

                lag = 2 * (1 - core)

                @pl.when((n >= lag) & (n < steps + lag))
                def _():
                    crossing(1, n - lag)

        @pl.when(n == 0)
        def _():
            tile(0, 1, wide - 1, WIDE, 1.0)

        loop(0, 3, lambda j: plain(n, j))

        @pl.when(n == 0)
        def _():
            loop(0, wide, lambda m: loss_tile(1, m))

        @pl.when((n == 1) & (core == 1))
        def _():
            loop(0, chunks, lambda c: arrived(0, 5, c))
            loop(0, wide, lambda m: loss_tile(5, m))

    def finish(side, out):
        def part(c):
            span = pl.ds(pl.multiple_of(c * CHUNK, CHUNK), CHUNK)
            scale = inv[side, span][:, :1]
            zn = raw[side, span].astype(jnp.float32) * scale
            grad = temp * d[side, span]
            out[span] = (grad - zn * jnp.sum(zn * grad, axis=1, keepdims=True)) * scale

        loop(0, chunks, part)

    finish(1, g_image)

    @pl.when(core == 0)
    def _():
        crossing(1, steps - 1)

    finish(0, g_text)

    def sent(side, kind, count):
        span = z.at[side, 0, pl.ds(0, count * CHUNK)]
        pltpu.make_async_remote_copy(
            src_ref=span, dst_ref=span, send_sem=send_sem.at[side, kind], recv_sem=recv_sem.at[side, 0, 0],
            device_id=partner, device_id_type=MESH,
        ).wait_send()

    for side in (0, 1):
        for kind in range(3):
            sent(side, kind, chunks)

        @pl.when((core == side) | (p == side))
        def _():
            sent(side, 3, chunks)

        @pl.when((core != side) & (p != side))
        def _():
            sent(side, 3, chunks - SPLIT)

        @pl.when((core != side) & (p == side))
        def _():
            sent(side, 4, SPLIT)

    @pl.when(core == 0)
    def _():
        sent(0, 5, chunks)

    loss[0] = jnp.sum(gathered(1, pairs)) / (rows * n_outer * n_inner)


def body(image_emb, text_emb, positive, log_temp, bias):
    rows, width = image_emb.shape
    chunks = rows // CHUNK
    vmem, smem, hbm = (pl.BlockSpec(memory_space=m) for m in (pltpu.VMEM, pltpu.SMEM, pltpu.HBM))
    large = (image_emb, text_emb, positive.reshape(1, rows))
    flops = 2 * 21 * rows * rows * width
    return pl.pallas_call(
        kernel,
        out_shape=(
            jax.ShapeDtypeStruct((1,), jnp.float32),
            pltpu.VMEM((rows, width), jnp.float32),
            pltpu.VMEM((rows, width), jnp.float32),
        ),
        in_specs=[hbm, hbm, hbm, smem, smem],
        out_specs=(smem, vmem, vmem),
        scratch_shapes=[
            pltpu.VMEM((2, 6, rows, width), jnp.bfloat16),
            pltpu.VMEM((2, rows, width), jnp.bfloat16),
            pltpu.VMEM((2, rows, width), jnp.float32),
            pltpu.VMEM((2, rows, 128), jnp.float32),
            pltpu.VMEM((8, 128), jnp.float32),
            pltpu.VMEM((2, 16, 8, 128), jnp.float32),
            pltpu.VMEM((1, rows), jnp.int32),
            pltpu.SemaphoreType.DMA((3, chunks)),
            pltpu.SemaphoreType.DMA((2, 6)),
            pltpu.SemaphoreType.DMA((2, 6, chunks)),
            pltpu.SemaphoreType.DMA((2,)),
            pltpu.SemaphoreType.DMA((2,)),
        ],
        compiler_params=pltpu.CompilerParams(
            collective_id=0, has_side_effects=True, vmem_limit_bytes=40 * 2**20
        ),
        cost_estimate=pl.CostEstimate(
            flops=flops, bytes_accessed=12 * rows * width, transcendentals=27 * rows * rows
        ),
        name="exchange",
    )(*(pltpu.with_memory_space_constraint(x, pltpu.HBM) for x in large), log_temp, bias)


def solution(mesh):
    placed = (
        P(("outer", "inner"), None),
        P(("outer", "inner"), None),
        P(("outer", "inner")),
        P(),
        P(),
    )
    return jax.shard_map(
        body,
        mesh=mesh,
        in_specs=placed,
        out_specs=(P(), P(("outer", "inner"), None), P(("outer", "inner"), None)),
        check_vma=False,
    )
```

```python
import functools

import jax
import jax.numpy as jnp
from jax import lax
from jax.experimental import pallas as pl
from jax.experimental.pallas import tpu as pltpu
from jax.sharding import PartitionSpec as P

MESH = pl.DeviceIdType.MESH
CHUNK = 64
WIDE, NARROW = 256, 128
HELD = 2
SPLIT = 4


def kernel(
    image, text, positive_hbm, log_temp, bias, loss, g_image, g_text,
    z, raw, d, inv, acc, terms, positive, load_sem, send_sem, recv_sem, loss_send, loss_recv,
):
    rows, width = image.shape
    chunks = rows // CHUNK
    n_outer, n_inner = lax.axis_size("outer"), lax.axis_size("inner")
    o, i = lax.axis_index("outer"), lax.axis_index("inner")
    p, core = lax.rem(i, 2), lax.rem(o, 2)

    def along(steps):
        return (o, lax.rem(i + steps + n_inner, n_inner))

    partner = (o, i + 1 - 2 * p)

    def across(side):
        return (
            lax.rem(o + 1 - 2 * side + n_outer, n_outer),
            lax.rem(i + core - side + n_inner, n_inner),
        )

    barrier = pltpu.get_barrier_semaphore()
    sibling = (o + 1 - 2 * core, i)
    between = (lax.rem(o + 2 * core - 1 + n_outer, n_outer), lax.rem(i + 1 - 2 * core + n_inner, n_inner))
    others = (along(2), along(-2), partner, across(0), across(1), between, sibling)

    group = 2 * n_inner
    pairs = n_outer // 2

    def near(k):
        m = lax.rem(2 * i + core + k, group)
        return (o - core + lax.rem(m, 2), m // 2)

    def far(k):
        return (lax.rem(o + 2 * k, n_outer), i)

    def loop(lower, upper, step):
        lax.fori_loop(lower, upper, lambda k, carry: (step(k), carry)[1], 0)

    def greet(device):
        pl.semaphore_signal(barrier, inc=1, device_id=device, device_id_type=MESH)

    for other in others:
        greet(other)
    loop(1, group, lambda k: greet(near(k)))
    loop(1, pairs, lambda k: greet(far(k)))
    n_greet = len(others) + group - 1 + pairs - 1

    def loading(side, c):
        source = image if side else text
        span = pl.ds(c * CHUNK, CHUNK)
        return pltpu.make_async_copy(source.at[span], raw.at[side, span], load_sem.at[side, c])

    for c in range(chunks):
        for side in (0, 1):
            loading(side, c).start()
    load_positive = pltpu.make_async_copy(positive_hbm, positive, load_sem.at[2, 0])
    load_positive.start()

    def copy(side, source, target, c, kind, device):
        span = pl.ds(c * CHUNK, CHUNK)
        return pltpu.make_async_remote_copy(
            src_ref=z.at[side, source, span],
            dst_ref=z.at[side, target, span],
            send_sem=send_sem.at[side, kind],
            recv_sem=recv_sem.at[side, target, c],
            device_id=device,
            device_id_type=MESH,
        )

    def send_ring(side, c):
        copy(side, 0, 2, c, 0, along(2 - 4 * side)).start()

    def send_partner(side, source, c):
        copy(side, source, 1, c, 1, partner).start()

    def send_on(side, c):
        copy(side, 1, 3, c, 2, along(2 - 4 * side)).start()

    def send_cross(side, source, c):
        copy(side, source, 4, c, 3, across(side)).start()

    def send_between(side, c):
        copy(side, 2, 6, c, 4, between).start()

    def pass_on(side, c):
        arrived(side, 6, c)
        copy(side, 6, 4, c, 6, along(2 - 4 * side)).start()

    def send_sibling(c):
        copy(0, 1, 5, c, 5, sibling).start()

    def arrived(side, slot, c):
        copy(side, slot, slot, c, 0, partner).wait_recv()

    def normalize(side, c):
        span = pl.ds(c * CHUNK, CHUNK)
        x = raw[side, span].astype(jnp.float32)
        scale = lax.rsqrt(jnp.sum(x * x, axis=1, keepdims=True) + 1e-06)
        inv[side, span] = jnp.broadcast_to(scale, (CHUNK, 128))
        z[side, 0, span] = (x * scale).astype(jnp.bfloat16)

    for c in range(chunks):
        for side in (0, 1):
            loading(side, c).wait()
            normalize(side, c)
            if c == 0 and side == 0:
                pl.semaphore_wait(barrier, n_greet)
            send_ring(side, c)
            if side == 0 or c < HELD:

                @pl.when(p == side)
                def _():
                    send_partner(side, 0, c)

    load_positive.wait()
    temp = jnp.exp(jnp.full((1, 128), log_temp[0], jnp.float32))[:, :1]
    shift = bias[0]

    def sigmoid_parts(logit):
        e = jnp.exp(-jnp.abs(logit))
        r = 1.0 / (1.0 + e)
        return e, jnp.where(logit >= 0.0, r, e * r)

    def fold(term):
        rest = jnp.sum(term.reshape(-1, 8, term.shape[1]), axis=0)
        return sum(rest[:, k:k + 128] for k in range(0, term.shape[1], 128))

    def term_copy(stage, k, device):
        return pltpu.make_async_remote_copy(
            src_ref=terms.at[stage, 0], dst_ref=terms.at[stage, k],
            send_sem=loss_send.at[stage], recv_sem=loss_recv.at[stage],
            device_id=device, device_id_type=MESH,
        )

    def spread(stage, value, count, where):
        terms[stage, 0] = value
        loop(1, count, lambda k: term_copy(stage, k, where(k)).start())

    def gathered(stage, count):
        block = terms.at[stage, pl.ds(1, count - 1)]
        both = pltpu.make_async_remote_copy(
            src_ref=block, dst_ref=block, send_sem=loss_send.at[stage], recv_sem=loss_recv.at[stage],
            device_id=partner, device_id_type=MESH,
        )
        both.wait_recv()
        both.wait_send()
        return jnp.sum(terms[stage, :count], axis=0)

    base = (o * n_inner + i) * rows
    acc[...] = jnp.zeros_like(acc)

    def own_tile(n, carry):
        span = pl.ds(pl.multiple_of(n * WIDE, WIDE), WIDE)
        scores = lax.dot_general(
            z[0, 0, span], z[1, 0], (((1,), (1,)), ((), ())), preferred_element_type=jnp.float32
        )
        logit = temp * scores + shift
        label = positive[...] - (base + n * WIDE) == lax.broadcasted_iota(jnp.int32, scores.shape, 0)
        e, sig = sigmoid_parts(logit)
        term = jnp.maximum(logit, 0.0) + jnp.log1p(e) - jnp.where(label, logit, 0.0)
        acc[...] += fold(term)
        coef = (sig - label.astype(jnp.float32)).astype(jnp.bfloat16)
        d[0, span] = jnp.dot(coef, z[1, 0], preferred_element_type=jnp.float32)
        add = lax.dot_general(
            coef, z[0, 0, span], (((0,), (0,)), ((), ())), preferred_element_type=jnp.float32
        )

        @pl.when(n == 0)
        def _():
            d[1] = add

        @pl.when(n > 0)
        def _():
            d[1] += add

        return carry

    lax.fori_loop(0, rows // WIDE, own_tile, 0)

    def softplus(logit, e):
        return fold(jnp.maximum(logit, 0.0) + jnp.log1p(e))

    def tile(side, slot, n, size, weight=None):
        span = pl.ds(pl.multiple_of(n * size, size), size)
        scores = lax.dot_general(
            z[1 - side, 0], z[side, slot, span], (((1,), (1,)), ((), ())),
            preferred_element_type=jnp.float32,
        )
        logit = temp * scores + shift
        e, sig = sigmoid_parts(logit)
        if weight is not None:
            acc[...] += weight * softplus(logit, e)
        d[1 - side] += jnp.dot(
            sig.astype(jnp.bfloat16), z[side, slot, span], preferred_element_type=jnp.float32
        )

    def loss_tile(slot, n):
        span = pl.ds(pl.multiple_of(n * WIDE, WIDE), WIDE)
        scores = lax.dot_general(
            z[1, 2], z[0, slot, span], (((1,), (1,)), ((), ())), preferred_element_type=jnp.float32
        )
        logit = temp * scores + shift
        acc[...] += softplus(logit, jnp.exp(-jnp.abs(logit)))

    def take_ring(side, c):
        arrived(side, 2, c)

        @pl.when(p != side)
        def _():
            send_partner(side, 2, c)

        @pl.when((core != side) & ((p == side) | (c >= SPLIT)))
        def _():
            send_cross(side, 2, c)

        @pl.when((core != side) & (p != side) & (c < SPLIT))
        def _():
            send_between(side, c)

    def take_last(side, c):
        arrived(side, 3, c)

        @pl.when(core == side)
        def _():
            send_cross(side, 3, c)

    def take_image(c):
        arrived(1, 1, c)
        send_on(1, c)

    per = NARROW // CHUNK
    steps = rows // NARROW
    wide = rows // WIDE

    def take_text(c):
        arrived(0, 1, c)

        @pl.when(core == 0)
        def _():
            send_sibling(c)

    @functools.partial(loop, 0, steps)
    def _(n):
        for k in range(per):
            c = n * per + k
            take_ring(0, c)
            take_ring(1, c)

            @pl.when(c > 0)
            def _():
                take_text(c - 1)

        for side in (0, 1):

            @pl.when((core == side) & (p == side) & (n > 0) & (n <= SPLIT // per))
            def _():
                for k in range(per):
                    pass_on(side, (n - 1) * per + k)

        @pl.when(n == steps - 1)
        def _():
            @pl.when(p == 1)
            def _():
                loop(HELD, chunks, lambda c: send_partner(1, 0, c))

        @pl.when(lax.rem(n, steps // wide) == steps // wide - 1)
        def _():
            tile(0, 2, n // (steps // wide), WIDE, 1.0)
            tile(1, 2, n // (steps // wide), WIDE)

        @pl.when(n == steps // wide)
        def _():
            tile(0, 1, 0, WIDE, 1.0)

    loop(0, chunks - 1, lambda c: send_on(0, c))
    take_text(chunks - 1)
    send_on(0, chunks - 1)

    def plain(n, j):
        side, slot = jnp.where(j == 1, 0, 1), jnp.where(j == 0, 1, 3)

        @pl.when(((j > 0) & (n > 0)) | ((j == 0) & (n < steps)))
        def _():
            tile(side, slot, n - jnp.minimum(j, 1), NARROW)

    def crossing(side, n, weight=None):
        for k in range(per):
            arrived(side, 4, n * per + k)
        tile(side, 4, n, NARROW, weight)

    @functools.partial(loop, 0, steps + 1)
    def _(n):
        @pl.when(n == steps)
        def _():
            spread(1, gathered(0, group), pairs, far)

        for k in range(per):
            c = n * per + k

            @pl.when(n < steps)
            def _():
                take_image(c)

            @pl.when(n > 0)
            def _():
                take_last(0, c - per)
                take_last(1, c - per)

            if k == 0:

                @pl.when((n >= 2 * core) & (n < steps + 2 * core))
                def _():
                    crossing(0, n - 2 * core, 1.0 - core.astype(jnp.float32))

                @pl.when(n == steps - 1)
                def _():
                    spread(0, acc[...], group, near)

                lag = 2 * (1 - core)

                @pl.when((n >= lag) & (n < steps + lag))
                def _():
                    crossing(1, n - lag)

        @pl.when(n == 0)
        def _():
            tile(0, 1, wide - 1, WIDE, 1.0)

        loop(0, 3, lambda j: plain(n, j))

        @pl.when(n == 0)
        def _():
            loop(0, wide, lambda m: loss_tile(1, m))

        @pl.when((n == 1) & (core == 1))
        def _():
            loop(0, chunks, lambda c: arrived(0, 5, c))
            loop(0, wide, lambda m: loss_tile(5, m))

    def finish(side, out):
        def part(c):
            span = pl.ds(pl.multiple_of(c * CHUNK, CHUNK), CHUNK)
            scale = inv[side, span][:, :1]
            zn = raw[side, span].astype(jnp.float32) * scale
            grad = temp * d[side, span]
            out[span] = (grad - zn * jnp.sum(zn * grad, axis=1, keepdims=True)) * scale

        loop(0, chunks, part)

    @pl.when(core == 0)
    def _():
        finish(1, g_image)
        crossing(1, steps - 1)
        finish(0, g_text)

    @pl.when(core == 1)
    def _():
        finish(0, g_text)
        crossing(0, steps - 1)
        finish(1, g_image)

    def sent(side, kind, count):
        span = z.at[side, 0, pl.ds(0, count * CHUNK)]
        pltpu.make_async_remote_copy(
            src_ref=span, dst_ref=span, send_sem=send_sem.at[side, kind], recv_sem=recv_sem.at[side, 0, 0],
            device_id=partner, device_id_type=MESH,
        ).wait_send()

    for side in (0, 1):
        for kind in range(3):
            sent(side, kind, chunks)

        @pl.when((core == side) | (p == side))
        def _():
            sent(side, 3, chunks)

        @pl.when((core != side) & (p != side))
        def _():
            sent(side, 3, chunks - SPLIT)
            sent(side, 4, SPLIT)

        @pl.when((core == side) & (p == side))
        def _():
            sent(side, 6, SPLIT)

    @pl.when(core == 0)
    def _():
        sent(0, 5, chunks)

    loss[0] = jnp.sum(gathered(1, pairs)) / (rows * n_outer * n_inner)


def body(image_emb, text_emb, positive, log_temp, bias):
    rows, width = image_emb.shape
    chunks = rows // CHUNK
    vmem, smem, hbm = (pl.BlockSpec(memory_space=m) for m in (pltpu.VMEM, pltpu.SMEM, pltpu.HBM))
    large = (image_emb, text_emb, positive.reshape(1, rows))
    flops = 2 * 21 * rows * rows * width
    return pl.pallas_call(
        kernel,
        out_shape=(
            jax.ShapeDtypeStruct((1,), jnp.float32),
            pltpu.VMEM((rows, width), jnp.float32),
            pltpu.VMEM((rows, width), jnp.float32),
        ),
        in_specs=[hbm, hbm, hbm, smem, smem],
        out_specs=(smem, vmem, vmem),
        scratch_shapes=[
            pltpu.VMEM((2, 7, rows, width), jnp.bfloat16),
            pltpu.VMEM((2, rows, width), jnp.bfloat16),
            pltpu.VMEM((2, rows, width), jnp.float32),
            pltpu.VMEM((2, rows, 128), jnp.float32),
            pltpu.VMEM((8, 128), jnp.float32),
            pltpu.VMEM((2, 16, 8, 128), jnp.float32),
            pltpu.VMEM((1, rows), jnp.int32),
            pltpu.SemaphoreType.DMA((3, chunks)),
            pltpu.SemaphoreType.DMA((2, 7)),
            pltpu.SemaphoreType.DMA((2, 7, chunks)),
            pltpu.SemaphoreType.DMA((2,)),
            pltpu.SemaphoreType.DMA((2,)),
        ],
        compiler_params=pltpu.CompilerParams(
            collective_id=0, has_side_effects=True, vmem_limit_bytes=40 * 2**20
        ),
        cost_estimate=pl.CostEstimate(
            flops=flops, bytes_accessed=12 * rows * width, transcendentals=27 * rows * rows
        ),
        name="exchange",
    )(*(pltpu.with_memory_space_constraint(x, pltpu.HBM) for x in large), log_temp, bias)


def solution(mesh):
    placed = (
        P(("outer", "inner"), None),
        P(("outer", "inner"), None),
        P(("outer", "inner")),
        P(),
        P(),
    )
    return jax.shard_map(
        body,
        mesh=mesh,
        in_specs=placed,
        out_specs=(P(), P(("outer", "inner"), None), P(("outer", "inner"), None)),
        check_vma=False,
    )
```

```python
import functools

import jax
import jax.numpy as jnp
from jax import lax
from jax.experimental import pallas as pl
from jax.experimental.pallas import tpu as pltpu
from jax.sharding import PartitionSpec as P

MESH = pl.DeviceIdType.MESH
CHUNK = 64
WIDE, NARROW = 256, 128
HELD = 2
SPLIT = 4


def kernel(
    image, text, positive_hbm, scalars, total, d, raw, inv,
    z, acc, terms, positive, load_sem, send_sem, recv_sem, loss_send, loss_recv,
):
    rows, width = image.shape
    chunks = rows // CHUNK
    n_outer, n_inner = lax.axis_size("outer"), lax.axis_size("inner")
    o, i = lax.axis_index("outer"), lax.axis_index("inner")
    p, core = lax.rem(i, 2), lax.rem(o, 2)

    def along(steps):
        return (o, lax.rem(i + steps + n_inner, n_inner))

    partner = (o, i + 1 - 2 * p)

    def across(side):
        return (
            lax.rem(o + 1 - 2 * side + n_outer, n_outer),
            lax.rem(i + core - side + n_inner, n_inner),
        )

    barrier = pltpu.get_barrier_semaphore()
    sibling = (o + 1 - 2 * core, i)
    between = (lax.rem(o + 2 * core - 1 + n_outer, n_outer), lax.rem(i + 1 - 2 * core + n_inner, n_inner))
    others = (along(2), along(-2), partner, across(0), across(1), between, sibling)

    group = 2 * n_inner
    pairs = n_outer // 2

    def near(k):
        m = lax.rem(2 * i + core + k, group)
        return (o - core + lax.rem(m, 2), m // 2)

    def far(k):
        return (lax.rem(o + 2 * k, n_outer), i)

    def loop(lower, upper, step):
        lax.fori_loop(lower, upper, lambda k, carry: (step(k), carry)[1], 0)

    def greet(device):
        pl.semaphore_signal(barrier, inc=1, device_id=device, device_id_type=MESH)

    for other in others:
        greet(other)
    loop(1, group, lambda k: greet(near(k)))
    loop(1, pairs, lambda k: greet(far(k)))
    n_greet = len(others) + group - 1 + pairs - 1

    def loading(side, c):
        source = image if side else text
        span = pl.ds(c * CHUNK, CHUNK)
        return pltpu.make_async_copy(source.at[span], raw.at[side, span], load_sem.at[side, c])

    for c in range(chunks):
        for side in (0, 1):
            loading(side, c).start()
    load_positive = pltpu.make_async_copy(positive_hbm, positive, load_sem.at[2, 0])
    load_positive.start()

    def copy(side, source, target, c, kind, device):
        span = pl.ds(c * CHUNK, CHUNK)
        return pltpu.make_async_remote_copy(
            src_ref=z.at[side, source, span],
            dst_ref=z.at[side, target, span],
            send_sem=send_sem.at[side, kind],
            recv_sem=recv_sem.at[side, target, c],
            device_id=device,
            device_id_type=MESH,
        )

    def send_ring(side, c):
        copy(side, 0, 2, c, 0, along(2 - 4 * side)).start()

    def send_partner(side, source, c):
        copy(side, source, 1, c, 1, partner).start()

    def send_on(side, c):
        copy(side, 1, 3, c, 2, along(2 - 4 * side)).start()

    def send_cross(side, source, c):
        copy(side, source, 4, c, 3, across(side)).start()

    def send_between(side, c):
        copy(side, 2, 6, c, 4, between).start()

    def pass_on(side, c):
        arrived(side, 6, c)
        copy(side, 6, 4, c, 6, along(2 - 4 * side)).start()

    def send_sibling(c):
        copy(0, 1, 5, c, 5, sibling).start()

    def arrived(side, slot, c):
        copy(side, slot, slot, c, 0, partner).wait_recv()

    def normalize(side, c):
        span = pl.ds(c * CHUNK, CHUNK)
        x = raw[side, span].astype(jnp.float32)
        scale = lax.rsqrt(jnp.sum(x * x, axis=1, keepdims=True) + 1e-06)
        inv[side, span] = jnp.broadcast_to(scale, (CHUNK, 128))
        z[side, 0, span] = (x * scale).astype(jnp.bfloat16)

    for c in range(chunks):
        for side in (0, 1):
            loading(side, c).wait()
            normalize(side, c)
            if c == 0 and side == 0:
                pl.semaphore_wait(barrier, n_greet)
            send_ring(side, c)
            if side == 0 or c < HELD:

                @pl.when(p == side)
                def _():
                    send_partner(side, 0, c)

    load_positive.wait()
    temp, shift = jnp.exp(scalars[0:1, 0:1]), scalars[1:2, 0:1]

    def sigmoid_parts(logit):
        e = jnp.exp(-jnp.abs(logit))
        r = 1.0 / (1.0 + e)
        return e, jnp.where(logit >= 0.0, r, e * r)

    def fold(term):
        rest = jnp.sum(term.reshape(-1, 8, term.shape[1]), axis=0)
        return sum(rest[:, k:k + 128] for k in range(0, term.shape[1], 128))

    def term_copy(stage, k, device):
        return pltpu.make_async_remote_copy(
            src_ref=terms.at[stage, 0], dst_ref=terms.at[stage, k],
            send_sem=loss_send.at[stage], recv_sem=loss_recv.at[stage],
            device_id=device, device_id_type=MESH,
        )

    def spread(stage, value, count, where):
        terms[stage, 0] = value
        loop(1, count, lambda k: term_copy(stage, k, where(k)).start())

    def gathered(stage, count):
        block = terms.at[stage, pl.ds(1, count - 1)]
        both = pltpu.make_async_remote_copy(
            src_ref=block, dst_ref=block, send_sem=loss_send.at[stage], recv_sem=loss_recv.at[stage],
            device_id=partner, device_id_type=MESH,
        )
        both.wait_recv()
        both.wait_send()
        return jnp.sum(terms[stage, :count], axis=0)

    base = (o * n_inner + i) * rows
    acc[...] = jnp.zeros_like(acc)

    def own_tile(n, carry):
        span = pl.ds(pl.multiple_of(n * WIDE, WIDE), WIDE)
        scores = lax.dot_general(
            z[0, 0, span], z[1, 0], (((1,), (1,)), ((), ())), preferred_element_type=jnp.float32
        )
        logit = temp * scores + shift
        label = positive[...] - (base + n * WIDE) == lax.broadcasted_iota(jnp.int32, scores.shape, 0)
        e, sig = sigmoid_parts(logit)
        term = jnp.maximum(logit, 0.0) + jnp.log1p(e) - jnp.where(label, logit, 0.0)
        acc[...] += fold(term)
        coef = (sig - label.astype(jnp.float32)).astype(jnp.bfloat16)
        d[0, span] = jnp.dot(coef, z[1, 0], preferred_element_type=jnp.float32)
        add = lax.dot_general(
            coef, z[0, 0, span], (((0,), (0,)), ((), ())), preferred_element_type=jnp.float32
        )

        @pl.when(n == 0)
        def _():
            d[1] = add

        @pl.when(n > 0)
        def _():
            d[1] += add

        return carry

    lax.fori_loop(0, rows // WIDE, own_tile, 0)

    def softplus(logit, e):
        return fold(jnp.maximum(logit, 0.0) + jnp.log1p(e))

    def tile(side, slot, n, size, weight=None):
        span = pl.ds(pl.multiple_of(n * size, size), size)
        scores = lax.dot_general(
            z[1 - side, 0], z[side, slot, span], (((1,), (1,)), ((), ())),
            preferred_element_type=jnp.float32,
        )
        logit = temp * scores + shift
        e, sig = sigmoid_parts(logit)
        if weight is not None:
            acc[...] += weight * softplus(logit, e)
        d[1 - side] += jnp.dot(
            sig.astype(jnp.bfloat16), z[side, slot, span], preferred_element_type=jnp.float32
        )

    def loss_tile(slot, n):
        span = pl.ds(pl.multiple_of(n * WIDE, WIDE), WIDE)
        scores = lax.dot_general(
            z[1, 2], z[0, slot, span], (((1,), (1,)), ((), ())), preferred_element_type=jnp.float32
        )
        logit = temp * scores + shift
        acc[...] += softplus(logit, jnp.exp(-jnp.abs(logit)))

    def take_ring(side, c):
        arrived(side, 2, c)

        @pl.when(p != side)
        def _():
            send_partner(side, 2, c)

        @pl.when((core != side) & ((p == side) | (c >= SPLIT)))
        def _():
            send_cross(side, 2, c)

        @pl.when((core != side) & (p != side) & (c < SPLIT))
        def _():
            send_between(side, c)

    def take_last(side, c):
        arrived(side, 3, c)

        @pl.when(core == side)
        def _():
            send_cross(side, 3, c)

    def take_image(c):
        arrived(1, 1, c)
        send_on(1, c)

    per = NARROW // CHUNK
    steps = rows // NARROW
    wide = rows // WIDE

    def take_text(c):
        arrived(0, 1, c)

        @pl.when(core == 0)
        def _():
            send_sibling(c)

    @functools.partial(loop, 0, steps)
    def _(n):
        for k in range(per):
            c = n * per + k
            take_ring(0, c)
            take_ring(1, c)

            @pl.when(c > 0)
            def _():
                take_text(c - 1)

        for side in (0, 1):

            @pl.when((core == side) & (p == side) & (n > 0) & (n <= SPLIT // per))
            def _():
                for k in range(per):
                    pass_on(side, (n - 1) * per + k)

        @pl.when(n == steps - 1)
        def _():
            @pl.when(p == 1)
            def _():
                loop(HELD, chunks, lambda c: send_partner(1, 0, c))

        @pl.when(lax.rem(n, steps // wide) == steps // wide - 1)
        def _():
            tile(0, 2, n // (steps // wide), WIDE, 1.0)
            tile(1, 2, n // (steps // wide), WIDE)

        @pl.when(n == steps // wide)
        def _():
            tile(0, 1, 0, WIDE, 1.0)

    loop(0, chunks - 1, lambda c: send_on(0, c))
    take_text(chunks - 1)
    send_on(0, chunks - 1)

    def plain(n, j):
        side, slot = jnp.where(j == 1, 0, 1), jnp.where(j == 0, 1, 3)

        @pl.when(((j > 0) & (n > 0)) | ((j == 0) & (n < steps)))
        def _():
            tile(side, slot, n - jnp.minimum(j, 1), NARROW)

    def crossing(side, n, weight=None):
        for k in range(per):
            arrived(side, 4, n * per + k)
        tile(side, 4, n, NARROW, weight)

    @functools.partial(loop, 0, steps + 1)
    def _(n):
        for k in range(per):
            c = n * per + k

            @pl.when(n < steps)
            def _():
                take_image(c)

            @pl.when(n > 0)
            def _():
                take_last(0, c - per)
                take_last(1, c - per)

            if k == 0:
                @pl.when((n > 0) & (n <= steps // 2))
                def _():
                    loop(2 * n - 2, 2 * n, lambda m: crossing(core, m, 1.0 - core.astype(jnp.float32)))

                @pl.when(n == steps // 2)
                def _():
                    spread(0, acc[...], group, near)

                @pl.when(n >= 2)
                def _():
                    crossing(1 - core, n - 2)

        @pl.when(n == 0)
        def _():
            tile(0, 1, wide - 1, WIDE, 1.0)

        loop(0, 3, lambda j: plain(n, j))

        @pl.when(n == steps - 1)
        def _():
            spread(1, gathered(0, group), pairs, far)

        @pl.when(n == 0)
        def _():
            loop(0, wide, lambda m: loss_tile(1, m))

        @pl.when((n == 0) & (core == 1))
        def _():
            loop(0, chunks, lambda c: arrived(0, 5, c))
            loop(0, wide, lambda m: loss_tile(5, m))

    crossing(1 - core, steps - 1)

    def sent(side, kind, count):
        span = z.at[side, 0, pl.ds(0, count * CHUNK)]
        pltpu.make_async_remote_copy(
            src_ref=span, dst_ref=span, send_sem=send_sem.at[side, kind], recv_sem=recv_sem.at[side, 0, 0],
            device_id=partner, device_id_type=MESH,
        ).wait_send()

    for side in (0, 1):
        for kind in range(3):
            sent(side, kind, chunks)

        @pl.when((core == side) | (p == side))
        def _():
            sent(side, 3, chunks)

        @pl.when((core != side) & (p != side))
        def _():
            sent(side, 3, chunks - SPLIT)
            sent(side, 4, SPLIT)

        @pl.when((core == side) & (p == side))
        def _():
            sent(side, 6, SPLIT)

    @pl.when(core == 0)
    def _():
        sent(0, 5, chunks)

    total[...] = gathered(1, pairs)


def finish(images, scalars, total, d, raw, inv, loss, g_image, g_text, grads, sems):
    rows = d.shape[1]
    temp = jnp.exp(scalars[0:1, 0:1])
    copies = []
    for c in range(rows // NARROW):
        span = pl.ds(c * NARROW, NARROW)
        for side, out in ((0, g_text), (1, g_image)):
            scale = inv[side, span][:, :1]
            zn = raw[side, span].astype(jnp.float32) * scale
            grad = temp * d[side, span]
            grads[side, span] = (grad - zn * jnp.sum(zn * grad, axis=1, keepdims=True)) * scale
            copies.append(pltpu.make_async_copy(grads.at[side, span], out.at[span], sems.at[side, c]))
            copies[-1].start()
    loss[0] = jnp.sum(total[...]) / images
    for copy in copies:
        copy.wait()


def body(image_emb, text_emb, positive, log_temp, bias):
    rows, width = image_emb.shape
    chunks = rows // CHUNK
    vmem, smem, hbm = (pl.BlockSpec(memory_space=m) for m in (pltpu.VMEM, pltpu.SMEM, pltpu.HBM))
    large = (image_emb, text_emb, positive.reshape(1, rows))
    row = lax.broadcasted_iota(jnp.int32, (8, 128), 0)
    scalars = jnp.where(row == 0, log_temp[0], bias[0])
    sums = pl.pallas_call(
        kernel,
        out_shape=(
            pltpu.VMEM((8, 128), jnp.float32),
            pltpu.VMEM((2, rows, width), jnp.float32),
            pltpu.VMEM((2, rows, width), jnp.bfloat16),
            pltpu.VMEM((2, rows, 128), jnp.float32),
        ),
        in_specs=[hbm, hbm, hbm, vmem],
        out_specs=(vmem,) * 4,
        scratch_shapes=[
            pltpu.VMEM((2, 7, rows, width), jnp.bfloat16),
            pltpu.VMEM((8, 128), jnp.float32),
            pltpu.VMEM((2, 16, 8, 128), jnp.float32),
            pltpu.VMEM((1, rows), jnp.int32),
            pltpu.SemaphoreType.DMA((3, chunks)),
            pltpu.SemaphoreType.DMA((2, 7)),
            pltpu.SemaphoreType.DMA((2, 7, chunks)),
            pltpu.SemaphoreType.DMA((2,)),
            pltpu.SemaphoreType.DMA((2,)),
        ],
        compiler_params=pltpu.CompilerParams(
            collective_id=0, has_side_effects=True, vmem_limit_bytes=40 * 2**20
        ),
        cost_estimate=pl.CostEstimate(
            flops=2 * 21 * rows * rows * width, bytes_accessed=4 * rows * width, transcendentals=27 * rows * rows
        ),
        name="exchange",
    )(*(pltpu.with_memory_space_constraint(x, pltpu.HBM) for x in large), scalars)
    images = rows * lax.axis_size("outer") * lax.axis_size("inner")
    grad = jax.ShapeDtypeStruct((rows, width), jnp.float32)
    return pl.pallas_call(
        functools.partial(finish, images),
        out_shape=(jax.ShapeDtypeStruct((1,), jnp.float32), grad, grad),
        in_specs=[vmem] * 5,
        out_specs=(smem, hbm, hbm),
        scratch_shapes=[
            pltpu.VMEM((2, rows, width), jnp.float32),
            pltpu.SemaphoreType.DMA((2, chunks)),
        ],
        compiler_params=pltpu.CompilerParams(vmem_limit_bytes=16 * 2**20),
        cost_estimate=pl.CostEstimate(
            flops=14 * rows * width, bytes_accessed=8 * rows * width, transcendentals=0
        ),
        name="finish",
    )(scalars, *sums)


def solution(mesh):
    placed = (
        P(("outer", "inner"), None),
        P(("outer", "inner"), None),
        P(("outer", "inner")),
        P(),
        P(),
    )
    return jax.shard_map(
        body,
        mesh=mesh,
        in_specs=placed,
        out_specs=(P(), P(("outer", "inner"), None), P(("outer", "inner"), None)),
        check_vma=False,
    )
```

```python
import functools

import jax
import jax.numpy as jnp
from jax import lax
from jax.experimental import pallas as pl
from jax.experimental.pallas import tpu as pltpu
from jax.sharding import PartitionSpec as P

MESH = pl.DeviceIdType.MESH
CHUNK = 64
WIDE, NARROW = 256, 128
HELD = 2
SPLIT = 4


def kernel(
    image, text, positive_hbm, scalars, total, d, raw, inv,
    z, acc, terms, positive, load_sem, send_sem, recv_sem, loss_send, loss_recv,
):
    rows, width = image.shape
    chunks = rows // CHUNK
    n_outer, n_inner = lax.axis_size("outer"), lax.axis_size("inner")
    o, i = lax.axis_index("outer"), lax.axis_index("inner")
    p, core = lax.rem(i, 2), lax.rem(o, 2)

    def along(steps):
        return (o, lax.rem(i + steps + n_inner, n_inner))

    partner = (o, i + 1 - 2 * p)

    def across(side):
        return (
            lax.rem(o + 1 - 2 * side + n_outer, n_outer),
            lax.rem(i + core - side + n_inner, n_inner),
        )

    def loading(side, c):
        source = image if side else text
        span = pl.ds(c * CHUNK, CHUNK)
        return pltpu.make_async_copy(source.at[span], raw.at[side, span], load_sem.at[side, c])

    for c in range(chunks):
        for side in (0, 1):
            loading(side, c).start()
    load_positive = pltpu.make_async_copy(positive_hbm, positive, load_sem.at[2, 0])
    load_positive.start()

    barrier = pltpu.get_barrier_semaphore()
    sibling = (o + 1 - 2 * core, i)
    between = (lax.rem(o + 2 * core - 1 + n_outer, n_outer), lax.rem(i + 1 - 2 * core + n_inner, n_inner))
    others = (along(2), along(-2), partner, across(0), across(1), between, sibling)

    group = 2 * n_inner
    pairs = n_outer // 2

    def near(k):
        m = lax.rem(2 * i + core + k, group)
        return (o - core + lax.rem(m, 2), m // 2)

    def far(k):
        return (lax.rem(o + 2 * k, n_outer), i)

    def loop(lower, upper, step):
        lax.fori_loop(lower, upper, lambda k, carry: (step(k), carry)[1], 0)

    def greet(device):
        pl.semaphore_signal(barrier, inc=1, device_id=device, device_id_type=MESH)

    for other in others:
        greet(other)
    loop(1, group, lambda k: greet(near(k)))
    loop(1, pairs, lambda k: greet(far(k)))
    n_greet = len(others) + group - 1 + pairs - 1

    def copy(side, source, target, c, kind, device):
        span = pl.ds(c * CHUNK, CHUNK)
        return pltpu.make_async_remote_copy(
            src_ref=z.at[side, source, span],
            dst_ref=z.at[side, target, span],
            send_sem=send_sem.at[side, kind],
            recv_sem=recv_sem.at[side, target, c],
            device_id=device,
            device_id_type=MESH,
        )

    def send_ring(side, c):
        copy(side, 0, 2, c, 0, along(2 - 4 * side)).start()

    def send_partner(side, source, c):
        copy(side, source, 1, c, 1, partner).start()

    def send_on(side, c):
        copy(side, 1, 3, c, 2, along(2 - 4 * side)).start()

    def send_cross(side, source, c):
        copy(side, source, 4, c, 3, across(side)).start()

    def send_between(side, c):
        copy(side, 2, 6, c, 4, between).start()

    def pass_on(side, c):
        arrived(side, 6, c)
        copy(side, 6, 4, c, 6, along(2 - 4 * side)).start()

    def send_sibling(c):
        copy(0, 1, 5, c, 5, sibling).start()

    def arrived(side, slot, c):
        copy(side, slot, slot, c, 0, partner).wait_recv()

    def normalize(side, c):
        span = pl.ds(c * CHUNK, CHUNK)
        x = raw[side, span].astype(jnp.float32)
        scale = lax.rsqrt(jnp.sum(x * x, axis=1, keepdims=True) + 1e-06)
        inv[side, span] = jnp.broadcast_to(scale, (CHUNK, 128))
        z[side, 0, span] = (x * scale).astype(jnp.bfloat16)

    for c in range(chunks):
        for side in (0, 1):
            loading(side, c).wait()
            normalize(side, c)
            if c == 0 and side == 0:
                pl.semaphore_wait(barrier, n_greet)
            send_ring(side, c)
            if side == 0 or c < HELD:

                @pl.when(p == side)
                def _():
                    send_partner(side, 0, c)

    load_positive.wait()
    temp, shift = jnp.exp(scalars[0:1, 0:1]), scalars[1:2, 0:1]

    def sigmoid_parts(logit):
        e = jnp.exp(-jnp.abs(logit))
        r = 1.0 / (1.0 + e)
        return e, jnp.where(logit >= 0.0, r, e * r)

    def fold(term):
        rest = jnp.sum(term.reshape(-1, 8, term.shape[1]), axis=0)
        return sum(rest[:, k:k + 128] for k in range(0, term.shape[1], 128))

    def term_copy(stage, k, device):
        return pltpu.make_async_remote_copy(
            src_ref=terms.at[stage, 0], dst_ref=terms.at[stage, k],
            send_sem=loss_send.at[stage], recv_sem=loss_recv.at[stage],
            device_id=device, device_id_type=MESH,
        )

    def spread(stage, value, count, where):
        terms[stage, 0] = value
        loop(1, count, lambda k: term_copy(stage, k, where(k)).start())

    def gathered(stage, count):
        block = terms.at[stage, pl.ds(1, count - 1)]
        both = pltpu.make_async_remote_copy(
            src_ref=block, dst_ref=block, send_sem=loss_send.at[stage], recv_sem=loss_recv.at[stage],
            device_id=partner, device_id_type=MESH,
        )
        both.wait_recv()
        both.wait_send()
        return jnp.sum(terms[stage, :count], axis=0)

    base = (o * n_inner + i) * rows
    acc[...] = jnp.zeros_like(acc)

    def own_tile(n, carry):
        span = pl.ds(pl.multiple_of(n * WIDE, WIDE), WIDE)
        scores = lax.dot_general(
            z[0, 0, span], z[1, 0], (((1,), (1,)), ((), ())), preferred_element_type=jnp.float32
        )
        logit = temp * scores + shift
        label = positive[...] - (base + n * WIDE) == lax.broadcasted_iota(jnp.int32, scores.shape, 0)
        e, sig = sigmoid_parts(logit)
        term = jnp.maximum(logit, 0.0) + jnp.log1p(e) - jnp.where(label, logit, 0.0)
        acc[...] += fold(term)
        coef = (sig - label.astype(jnp.float32)).astype(jnp.bfloat16)
        d[0, span] = jnp.dot(coef, z[1, 0], preferred_element_type=jnp.float32)
        add = lax.dot_general(
            coef, z[0, 0, span], (((0,), (0,)), ((), ())), preferred_element_type=jnp.float32
        )

        @pl.when(n == 0)
        def _():
            d[1] = add

        @pl.when(n > 0)
        def _():
            d[1] += add

        return carry

    lax.fori_loop(0, rows // WIDE, own_tile, 0)

    def softplus(logit, e):
        return fold(jnp.maximum(logit, 0.0) + jnp.log1p(e))

    def tile(side, slot, n, size, weight=None):
        span = pl.ds(pl.multiple_of(n * size, size), size)
        meet(side, z[side, slot, span], weight)

    def meet(side, block, weight=None):
        scores = lax.dot_general(
            z[1 - side, 0], block, (((1,), (1,)), ((), ())), preferred_element_type=jnp.float32
        )
        logit = temp * scores + shift
        e, sig = sigmoid_parts(logit)
        if weight is not None:
            acc[...] += weight * softplus(logit, e)
        d[1 - side] += jnp.dot(sig.astype(jnp.bfloat16), block, preferred_element_type=jnp.float32)

    def loss_tile(slot, n):
        span = pl.ds(pl.multiple_of(n * WIDE, WIDE), WIDE)
        scores = lax.dot_general(
            z[1, 2], z[0, slot, span], (((1,), (1,)), ((), ())), preferred_element_type=jnp.float32
        )
        logit = temp * scores + shift
        acc[...] += softplus(logit, jnp.exp(-jnp.abs(logit)))

    def take_ring(side, c):
        arrived(side, 2, c)

        @pl.when(p != side)
        def _():
            send_partner(side, 2, c)

        @pl.when((core != side) & ((p == side) | (c >= SPLIT)))
        def _():
            send_cross(side, 2, c)

        @pl.when((core != side) & (p != side) & (c < SPLIT))
        def _():
            send_between(side, c)

    def take_last(side, c):
        arrived(side, 3, c)

        @pl.when(core == side)
        def _():
            send_cross(side, 3, c)

    def take_image(c):
        arrived(1, 1, c)
        send_on(1, c)

    per = NARROW // CHUNK
    steps = rows // NARROW
    wide = rows // WIDE

    def take_text(c):
        arrived(0, 1, c)

        @pl.when(core == 0)
        def _():
            send_sibling(c)

    @functools.partial(loop, 0, steps)
    def _(n):
        for k in range(per):
            c = n * per + k
            take_ring(0, c)
            take_ring(1, c)

            @pl.when(c > 0)
            def _():
                take_text(c - 1)

        for side in (0, 1):

            @pl.when((core == side) & (p == side) & (n > 0) & (n <= SPLIT // per))
            def _():
                for k in range(per):
                    pass_on(side, (n - 1) * per + k)

        @pl.when(n == steps - 1)
        def _():
            @pl.when(p == 1)
            def _():
                loop(HELD, chunks, lambda c: send_partner(1, 0, c))

        @pl.when(lax.rem(n, steps // wide) == steps // wide - 1)
        def _():
            tile(0, 2, n // (steps // wide), WIDE, 1.0)
            tile(1, 2, n // (steps // wide), WIDE)

        @pl.when(n == steps // wide)
        def _():
            tile(0, 1, 0, WIDE, 1.0)

    loop(0, chunks - 1, lambda c: send_on(0, c))
    take_text(chunks - 1)
    send_on(0, chunks - 1)

    def plain(n, j):
        side, slot = jnp.where(j == 1, 0, 1), jnp.where(j == 0, 1, 3)

        @pl.when(jnp.where(j == 0, n < steps, (n > 0) & ((n < steps) | (side == core))))
        def _():
            tile(side, slot, n - jnp.minimum(j, 1), NARROW)

    def crossing(side, n, weight=None):
        for k in range(per):
            arrived(side, 4, n * per + k)
        tile(side, 4, n, NARROW, weight)

    @functools.partial(loop, 0, steps + 1)
    def _(n):
        for k in range(per):
            c = n * per + k

            @pl.when(n < steps)
            def _():
                take_image(c)

            @pl.when(n > 0)
            def _():
                take_last(0, c - per)
                take_last(1, c - per)

            if k == 0:
                @pl.when((n > 0) & (n <= steps // 2))
                def _():
                    loop(2 * n - 2, 2 * n, lambda m: crossing(core, m, 1.0 - core.astype(jnp.float32)))

                @pl.when(n == steps // 2)
                def _():
                    spread(0, acc[...], group, near)

                @pl.when(n >= 2)
                def _():
                    crossing(1 - core, n - 2)

        @pl.when(n == 0)
        def _():
            tile(0, 1, wide - 1, WIDE, 1.0)

        loop(0, 3, lambda j: plain(n, j))

        @pl.when(n == steps - 1)
        def _():
            spread(1, gathered(0, group), pairs, far)

        @pl.when(n == 0)
        def _():
            loop(0, wide, lambda m: loss_tile(1, m))

        @pl.when((n == 0) & (core == 1))
        def _():
            loop(0, chunks, lambda c: arrived(0, 5, c))
            loop(0, wide, lambda m: loss_tile(5, m))

    for k in range(per):
        arrived(1 - core, 4, chunks - per + k)
    span = pl.ds(rows - NARROW, NARROW)
    meet(1 - core, jnp.concatenate([z[1 - core, 3, span], z[1 - core, 4, span]], axis=0))

    def sent(side, kind, count):
        span = z.at[side, 0, pl.ds(0, count * CHUNK)]
        pltpu.make_async_remote_copy(
            src_ref=span, dst_ref=span, send_sem=send_sem.at[side, kind], recv_sem=recv_sem.at[side, 0, 0],
            device_id=partner, device_id_type=MESH,
        ).wait_send()

    for side in (0, 1):
        for kind in range(3):
            sent(side, kind, chunks)

        @pl.when((core == side) | (p == side))
        def _():
            sent(side, 3, chunks)

        @pl.when((core != side) & (p != side))
        def _():
            sent(side, 3, chunks - SPLIT)
            sent(side, 4, SPLIT)

        @pl.when((core == side) & (p == side))
        def _():
            sent(side, 6, SPLIT)

    @pl.when(core == 0)
    def _():
        sent(0, 5, chunks)

    total[...] = gathered(1, pairs)


def finish(images, scalars, total, d, raw, inv, loss, g_image, g_text, grads, sems):
    rows = d.shape[1]
    temp = jnp.exp(scalars[0:1, 0:1])
    copies = []
    for c in range(rows // NARROW):
        span = pl.ds(c * NARROW, NARROW)
        for side, out in ((0, g_text), (1, g_image)):
            scale = inv[side, span][:, :1]
            zn = raw[side, span].astype(jnp.float32) * scale
            grad = temp * d[side, span]
            grads[side, span] = (grad - zn * jnp.sum(zn * grad, axis=1, keepdims=True)) * scale
            copies.append(pltpu.make_async_copy(grads.at[side, span], out.at[span], sems.at[side, c]))
            copies[-1].start()
    loss[0] = jnp.sum(total[...]) / images
    for copy in copies:
        copy.wait()


def body(image_emb, text_emb, positive, log_temp, bias):
    rows, width = image_emb.shape
    chunks = rows // CHUNK
    vmem, smem, hbm = (pl.BlockSpec(memory_space=m) for m in (pltpu.VMEM, pltpu.SMEM, pltpu.HBM))
    large = (image_emb, text_emb, positive.reshape(1, rows))
    row = lax.broadcasted_iota(jnp.int32, (8, 128), 0)
    scalars = jnp.where(row == 0, log_temp[0], bias[0])
    sums = pl.pallas_call(
        kernel,
        out_shape=(
            pltpu.VMEM((8, 128), jnp.float32),
            pltpu.VMEM((2, rows, width), jnp.float32),
            pltpu.VMEM((2, rows, width), jnp.bfloat16),
            pltpu.VMEM((2, rows, 128), jnp.float32),
        ),
        in_specs=[hbm, hbm, hbm, vmem],
        out_specs=(vmem,) * 4,
        scratch_shapes=[
            pltpu.VMEM((2, 7, rows, width), jnp.bfloat16),
            pltpu.VMEM((8, 128), jnp.float32),
            pltpu.VMEM((2, 16, 8, 128), jnp.float32),
            pltpu.VMEM((1, rows), jnp.int32),
            pltpu.SemaphoreType.DMA((3, chunks)),
            pltpu.SemaphoreType.DMA((2, 7)),
            pltpu.SemaphoreType.DMA((2, 7, chunks)),
            pltpu.SemaphoreType.DMA((2,)),
            pltpu.SemaphoreType.DMA((2,)),
        ],
        compiler_params=pltpu.CompilerParams(
            collective_id=0, has_side_effects=True, vmem_limit_bytes=40 * 2**20
        ),
        cost_estimate=pl.CostEstimate(
            flops=2 * 21 * rows * rows * width, bytes_accessed=4 * rows * width, transcendentals=27 * rows * rows
        ),
        name="exchange",
    )(*(pltpu.with_memory_space_constraint(x, pltpu.HBM) for x in large), scalars)
    images = rows * lax.axis_size("outer") * lax.axis_size("inner")
    grad = jax.ShapeDtypeStruct((rows, width), jnp.float32)
    return pl.pallas_call(
        functools.partial(finish, images),
        out_shape=(jax.ShapeDtypeStruct((1,), jnp.float32), grad, grad),
        in_specs=[vmem] * 5,
        out_specs=(smem, hbm, hbm),
        scratch_shapes=[
            pltpu.VMEM((2, rows, width), jnp.float32),
            pltpu.SemaphoreType.DMA((2, chunks)),
        ],
        compiler_params=pltpu.CompilerParams(vmem_limit_bytes=16 * 2**20),
        cost_estimate=pl.CostEstimate(
            flops=14 * rows * width, bytes_accessed=8 * rows * width, transcendentals=0
        ),
        name="finish",
    )(scalars, *sums)


def solution(mesh):
    placed = (
        P(("outer", "inner"), None),
        P(("outer", "inner"), None),
        P(("outer", "inner")),
        P(),
        P(),
    )
    return jax.shard_map(
        body,
        mesh=mesh,
        in_specs=placed,
        out_specs=(P(), P(("outer", "inner"), None), P(("outer", "inner"), None)),
        check_vma=False,
    )
```

```python
import functools

import jax
import jax.numpy as jnp
from jax import lax
from jax.experimental import pallas as pl
from jax.experimental.pallas import tpu as pltpu
from jax.sharding import PartitionSpec as P

MESH = pl.DeviceIdType.MESH
CHUNK = 64
WIDE, NARROW = 256, 128
HELD = 2
SPLIT = 4


def kernel(
    image, text, positive_hbm, scalars, total, d, raw, inv,
    z, acc, terms, positive, load_sem, send_sem, recv_sem, loss_send, loss_recv,
):
    rows, width = image.shape
    chunks = rows // CHUNK
    n_outer, n_inner = lax.axis_size("outer"), lax.axis_size("inner")
    o, i = lax.axis_index("outer"), lax.axis_index("inner")
    p, core = lax.rem(i, 2), lax.rem(o, 2)

    def along(steps):
        return (o, lax.rem(i + steps + n_inner, n_inner))

    partner = (o, i + 1 - 2 * p)

    def across(side):
        return (
            lax.rem(o + 1 - 2 * side + n_outer, n_outer),
            lax.rem(i + core - side + n_inner, n_inner),
        )

    def loading(side, c):
        source = image if side else text
        span = pl.ds(c * CHUNK, CHUNK)
        return pltpu.make_async_copy(source.at[span], raw.at[side, span], load_sem.at[side, c])

    for c in range(chunks):
        for side in (0, 1):
            loading(side, c).start()
    load_positive = pltpu.make_async_copy(positive_hbm, positive, load_sem.at[2, 0])
    load_positive.start()

    barrier = pltpu.get_barrier_semaphore()
    sibling = (o + 1 - 2 * core, i)
    between = (lax.rem(o + 2 * core - 1 + n_outer, n_outer), lax.rem(i + 1 - 2 * core + n_inner, n_inner))
    others = (along(2), along(-2), partner, across(0), across(1), between, sibling)

    group = 2 * n_inner
    pairs = n_outer // 2

    def near(k):
        m = lax.rem(2 * i + core + k, group)
        return (o - core + lax.rem(m, 2), m // 2)

    def far(k):
        return (lax.rem(o + 2 * k, n_outer), i)

    def loop(lower, upper, step):
        lax.fori_loop(lower, upper, lambda k, carry: (step(k), carry)[1], 0)

    def greet(device):
        pl.semaphore_signal(barrier, inc=1, device_id=device, device_id_type=MESH)

    for other in others:
        greet(other)
    loop(1, group, lambda k: greet(near(k)))
    loop(1, pairs, lambda k: greet(far(k)))
    n_greet = len(others) + group - 1 + pairs - 1

    def copy(side, source, target, c, kind, device):
        span = pl.ds(c * CHUNK, CHUNK)
        return pltpu.make_async_remote_copy(
            src_ref=z.at[side, source, span],
            dst_ref=z.at[side, target, span],
            send_sem=send_sem.at[side, kind],
            recv_sem=recv_sem.at[side, target, c],
            device_id=device,
            device_id_type=MESH,
        )

    def send_ring(side, c):
        copy(side, 0, 2, c, 0, along(2 - 4 * side)).start()

    def send_partner(side, source, c):
        copy(side, source, 1, c, 1, partner).start()

    def send_on(side, c):
        copy(side, 1, 3, c, 2, along(2 - 4 * side)).start()

    def send_cross(side, source, c):
        copy(side, source, 4, c, 3, across(side)).start()

    def send_between(side, c):
        copy(side, 2, 6, c, 4, between).start()

    def pass_on(side, c):
        arrived(side, 6, c)
        copy(side, 6, 4, c, 6, along(2 - 4 * side)).start()

    def send_sibling(c):
        copy(0, 1, 5, c, 5, sibling).start()

    def arrived(side, slot, c):
        copy(side, slot, slot, c, 0, partner).wait_recv()

    def normalize(side, c):
        span = pl.ds(c * CHUNK, CHUNK)
        x = raw[side, span].astype(jnp.float32)
        scale = lax.rsqrt(jnp.sum(x * x, axis=1, keepdims=True) + 1e-06)
        inv[side, span] = jnp.broadcast_to(scale, (CHUNK, 128))
        z[side, 0, span] = (x * scale).astype(jnp.bfloat16)

    for c in range(chunks):
        for side in (0, 1):
            loading(side, c).wait()
            normalize(side, c)
            if c == 0 and side == 0:
                pl.semaphore_wait(barrier, n_greet)
            send_ring(side, c)
            if side == 0 or c < HELD:

                @pl.when(p == side)
                def _():
                    send_partner(side, 0, c)

    load_positive.wait()
    temp, shift = jnp.exp(scalars[0:1, 0:1]), scalars[1:2, 0:1]

    def sigmoid_parts(logit):
        e = jnp.exp(-jnp.abs(logit))
        r = 1.0 / (1.0 + e)
        return e, jnp.where(logit >= 0.0, r, e * r)

    def fold(term):
        rest = jnp.sum(term.reshape(-1, 8, term.shape[1]), axis=0)
        return sum(rest[:, k:k + 128] for k in range(0, term.shape[1], 128))

    def term_copy(stage, k, device):
        return pltpu.make_async_remote_copy(
            src_ref=terms.at[stage, 0], dst_ref=terms.at[stage, k],
            send_sem=loss_send.at[stage], recv_sem=loss_recv.at[stage],
            device_id=device, device_id_type=MESH,
        )

    def spread(stage, value, count, where):
        terms[stage, 0] = value
        loop(1, count, lambda k: term_copy(stage, k, where(k)).start())

    def gathered(stage, count):
        block = terms.at[stage, pl.ds(1, count - 1)]
        both = pltpu.make_async_remote_copy(
            src_ref=block, dst_ref=block, send_sem=loss_send.at[stage], recv_sem=loss_recv.at[stage],
            device_id=partner, device_id_type=MESH,
        )
        both.wait_recv()
        both.wait_send()
        return jnp.sum(terms[stage, :count], axis=0)

    base = (o * n_inner + i) * rows
    acc[...] = jnp.zeros_like(acc)

    def own_tile(n, carry):
        span = pl.ds(pl.multiple_of(n * WIDE, WIDE), WIDE)
        scores = lax.dot_general(
            z[0, 0, span], z[1, 0], (((1,), (1,)), ((), ())), preferred_element_type=jnp.float32
        )
        logit = temp * scores + shift
        label = positive[...] - (base + n * WIDE) == lax.broadcasted_iota(jnp.int32, scores.shape, 0)
        e, sig = sigmoid_parts(logit)
        term = jnp.maximum(logit, 0.0) + jnp.log1p(e) - jnp.where(label, logit, 0.0)
        acc[...] += fold(term)
        coef = (sig - label.astype(jnp.float32)).astype(jnp.bfloat16)
        d[0, span] = jnp.dot(coef, z[1, 0], preferred_element_type=jnp.float32)
        add = lax.dot_general(
            coef, z[0, 0, span], (((0,), (0,)), ((), ())), preferred_element_type=jnp.float32
        )

        @pl.when(n == 0)
        def _():
            d[1] = add

        @pl.when(n > 0)
        def _():
            d[1] += add

        return carry

    lax.fori_loop(0, rows // WIDE, own_tile, 0)

    def softplus(logit, e):
        return fold(jnp.maximum(logit, 0.0) + jnp.log1p(e))

    def tile(side, slot, n, size, weight=None):
        span = pl.ds(pl.multiple_of(n * size, size), size)
        meet(side, z[side, slot, span], weight)

    def meet(side, block, weight=None):
        scores = lax.dot_general(
            z[1 - side, 0], block, (((1,), (1,)), ((), ())), preferred_element_type=jnp.float32
        )
        logit = temp * scores + shift
        e, sig = sigmoid_parts(logit)
        if weight is not None:
            acc[...] += weight * softplus(logit, e)
        d[1 - side] += jnp.dot(sig.astype(jnp.bfloat16), block, preferred_element_type=jnp.float32)

    def loss_tile(slot, n):
        span = pl.ds(pl.multiple_of(n * WIDE, WIDE), WIDE)
        scores = lax.dot_general(
            z[1, 2], z[0, slot, span], (((1,), (1,)), ((), ())), preferred_element_type=jnp.float32
        )
        logit = temp * scores + shift
        acc[...] += softplus(logit, jnp.exp(-jnp.abs(logit)))

    def take_ring(side, c):
        arrived(side, 2, c)

        @pl.when(p != side)
        def _():
            send_partner(side, 2, c)

        @pl.when((core != side) & ((p == side) | (c >= SPLIT)))
        def _():
            send_cross(side, 2, c)

        @pl.when((core != side) & (p != side) & (c < SPLIT))
        def _():
            send_between(side, c)

    def take_last(side, c):
        arrived(side, 3, c)

        @pl.when(core == side)
        def _():
            send_cross(side, 3, c)

    def take_image(c):
        arrived(1, 1, c)
        send_on(1, c)

    per = NARROW // CHUNK
    steps = rows // NARROW
    wide = rows // WIDE

    def take_text(c):
        arrived(0, 1, c)

        @pl.when(core == 0)
        def _():
            send_sibling(c)

    @functools.partial(loop, 0, steps)
    def _(n):
        for k in range(per):
            c = n * per + k
            take_ring(0, c)
            take_ring(1, c)

            @pl.when(c > 0)
            def _():
                take_text(c - 1)

        for side in (0, 1):

            @pl.when((core == side) & (p == side) & (n > 0) & (n <= SPLIT // per))
            def _():
                for k in range(per):
                    pass_on(side, (n - 1) * per + k)

        @pl.when(n == steps - 1)
        def _():
            @pl.when(p == 1)
            def _():
                loop(HELD, chunks, lambda c: send_partner(1, 0, c))

        @pl.when(lax.rem(n, steps // wide) == steps // wide - 1)
        def _():
            tile(0, 2, n // (steps // wide), WIDE, 1.0)
            tile(1, 2, n // (steps // wide), WIDE)

        @pl.when(n == steps // wide)
        def _():
            tile(0, 1, 0, WIDE, 1.0)

    loop(0, chunks - 1, lambda c: send_on(0, c))
    take_text(chunks - 1)
    send_on(0, chunks - 1)

    def plain(n, j):
        side, slot = jnp.where(j == 1, 0, 1), jnp.where(j == 0, 1, 3)

        last = (n == steps) & (side == core)

        @pl.when(jnp.where(j == 0, n == 0, last | ((j == 1) & (n > 0) & (n < steps))))
        def _():
            tile(side, slot, n - jnp.minimum(j, 1), NARROW)

    def crossing(side, n, weight=None):
        for k in range(per):
            arrived(side, 4, n * per + k)
        tile(side, 4, n, NARROW, weight)

    @functools.partial(loop, 0, steps + 1)
    def _(n):
        for k in range(per):
            c = n * per + k

            @pl.when(n < steps)
            def _():
                take_image(c)

            @pl.when(n > 0)
            def _():
                take_last(0, c - per)
                take_last(1, c - per)

            if k == 0:
                @pl.when((n > 0) & (n <= steps // 2))
                def _():
                    loop(2 * n - 2, 2 * n, lambda m: crossing(core, m, 1.0 - core.astype(jnp.float32)))

                @pl.when(n == steps // 2)
                def _():
                    spread(0, acc[...], group, near)

                @pl.when(n >= 2)
                def _():
                    crossing(1 - core, n - 2)

        @pl.when(n == 0)
        def _():
            tile(0, 1, wide - 1, WIDE, 1.0)

        loop(0, 3, lambda j: plain(n, j))

        @pl.when((n > 0) & (n < steps))
        def _():
            one, three = (pl.ds(pl.multiple_of((n - k) * NARROW, NARROW), NARROW) for k in (0, 1))
            meet(1, jnp.concatenate([z[1, 1, one], z[1, 3, three]], axis=0))

        @pl.when(n == steps - 1)
        def _():
            spread(1, gathered(0, group), pairs, far)

        @pl.when(n == 0)
        def _():
            loop(0, wide, lambda m: loss_tile(1, m))

        @pl.when((n == 0) & (core == 1))
        def _():
            loop(0, chunks, lambda c: arrived(0, 5, c))
            loop(0, wide, lambda m: loss_tile(5, m))

    for k in range(per):
        arrived(1 - core, 4, chunks - per + k)
    span = pl.ds(rows - NARROW, NARROW)
    meet(1 - core, jnp.concatenate([z[1 - core, 3, span], z[1 - core, 4, span]], axis=0))

    def sent(side, kind, count):
        span = z.at[side, 0, pl.ds(0, count * CHUNK)]
        pltpu.make_async_remote_copy(
            src_ref=span, dst_ref=span, send_sem=send_sem.at[side, kind], recv_sem=recv_sem.at[side, 0, 0],
            device_id=partner, device_id_type=MESH,
        ).wait_send()

    for side in (0, 1):
        for kind in range(3):
            sent(side, kind, chunks)

        @pl.when((core == side) | (p == side))
        def _():
            sent(side, 3, chunks)

        @pl.when((core != side) & (p != side))
        def _():
            sent(side, 3, chunks - SPLIT)
            sent(side, 4, SPLIT)

        @pl.when((core == side) & (p == side))
        def _():
            sent(side, 6, SPLIT)

    @pl.when(core == 0)
    def _():
        sent(0, 5, chunks)

    total[...] = gathered(1, pairs)


def finish(images, scalars, total, d, raw, inv, loss, g_image, g_text, grads, sems):
    rows = d.shape[1]
    temp = jnp.exp(scalars[0:1, 0:1])
    copies = []
    for c in range(rows // NARROW):
        span = pl.ds(c * NARROW, NARROW)
        for side, out in ((0, g_text), (1, g_image)):
            scale = inv[side, span][:, :1]
            zn = raw[side, span].astype(jnp.float32) * scale
            grad = temp * d[side, span]
            grads[side, span] = (grad - zn * jnp.sum(zn * grad, axis=1, keepdims=True)) * scale
            copies.append(pltpu.make_async_copy(grads.at[side, span], out.at[span], sems.at[side, c]))
            copies[-1].start()
    loss[0] = jnp.sum(total[...]) / images
    for copy in copies:
        copy.wait()


def body(image_emb, text_emb, positive, log_temp, bias):
    rows, width = image_emb.shape
    chunks = rows // CHUNK
    vmem, smem, hbm = (pl.BlockSpec(memory_space=m) for m in (pltpu.VMEM, pltpu.SMEM, pltpu.HBM))
    large = (image_emb, text_emb, positive.reshape(1, rows))
    row = lax.broadcasted_iota(jnp.int32, (8, 128), 0)
    scalars = jnp.where(row == 0, log_temp[0], bias[0])
    sums = pl.pallas_call(
        kernel,
        out_shape=(
            pltpu.VMEM((8, 128), jnp.float32),
            pltpu.VMEM((2, rows, width), jnp.float32),
            pltpu.VMEM((2, rows, width), jnp.bfloat16),
            pltpu.VMEM((2, rows, 128), jnp.float32),
        ),
        in_specs=[hbm, hbm, hbm, vmem],
        out_specs=(vmem,) * 4,
        scratch_shapes=[
            pltpu.VMEM((2, 7, rows, width), jnp.bfloat16),
            pltpu.VMEM((8, 128), jnp.float32),
            pltpu.VMEM((2, 16, 8, 128), jnp.float32),
            pltpu.VMEM((1, rows), jnp.int32),
            pltpu.SemaphoreType.DMA((3, chunks)),
            pltpu.SemaphoreType.DMA((2, 7)),
            pltpu.SemaphoreType.DMA((2, 7, chunks)),
            pltpu.SemaphoreType.DMA((2,)),
            pltpu.SemaphoreType.DMA((2,)),
        ],
        compiler_params=pltpu.CompilerParams(
            collective_id=0, has_side_effects=True, vmem_limit_bytes=40 * 2**20
        ),
        cost_estimate=pl.CostEstimate(
            flops=2 * 21 * rows * rows * width, bytes_accessed=4 * rows * width, transcendentals=27 * rows * rows
        ),
        name="exchange",
    )(*(pltpu.with_memory_space_constraint(x, pltpu.HBM) for x in large), scalars)
    images = rows * lax.axis_size("outer") * lax.axis_size("inner")
    grad = jax.ShapeDtypeStruct((rows, width), jnp.float32)
    return pl.pallas_call(
        functools.partial(finish, images),
        out_shape=(jax.ShapeDtypeStruct((1,), jnp.float32), grad, grad),
        in_specs=[vmem] * 5,
        out_specs=(smem, hbm, hbm),
        scratch_shapes=[
            pltpu.VMEM((2, rows, width), jnp.float32),
            pltpu.SemaphoreType.DMA((2, chunks)),
        ],
        compiler_params=pltpu.CompilerParams(vmem_limit_bytes=16 * 2**20),
        cost_estimate=pl.CostEstimate(
            flops=14 * rows * width, bytes_accessed=8 * rows * width, transcendentals=0
        ),
        name="finish",
    )(scalars, *sums)


def solution(mesh):
    placed = (
        P(("outer", "inner"), None),
        P(("outer", "inner"), None),
        P(("outer", "inner")),
        P(),
        P(),
    )
    return jax.shard_map(
        body,
        mesh=mesh,
        in_specs=placed,
        out_specs=(P(), P(("outer", "inner"), None), P(("outer", "inner"), None)),
        check_vma=False,
    )
```
